32 devices in a mesh: sub: 8 (over z, y), grp: 4 (over x, core).
Axes of the slice: x: 2, y: 2, z: 4, core: 2. Of those that a mesh axis runs over, the one named last changes fastest.
Arguments:
- rhs: float32 [8192, 512], P(('sub', 'grp')), may hold values from -120 to 120
- kappa: float32 [8192], P(('sub', 'grp')), may hold values from 0.5 to 5
- stiffness: float32 [512, 512], replicated, may hold values from -1 to 3
- local_inverse: float32 [512, 512], replicated, may hold values from -1 to 2
- modes: float32 [8, 512], replicated, may hold values from -0.25 to 0.25
- coarse_weight: float32 [8, 8192], P(None, ('sub', 'grp')), may hold values from 0.5 to 1.5
- coarse_mask: int32 [8, 8192], P(None, ('sub', 'grp')), may hold values 0 or 1
- coarse_inverse: float32 [256, 256], P(('sub', 'grp')), may hold values from -1 to 1
- neighbours: int32 [4, 8192], P(None, ('sub', 'grp')), may hold values from -1 to 8191, as said below
Outputs:
- solution: float32 [8192, 512], P(('sub', 'grp'))
The draws below stay inside these ranges and needn't reach their ends.
Inputs may be any that keep to these rules, and one draw needn't show every extreme that they name: `neighbours`: entries are element numbers or -1. For element e of subdomain d (elements d * 256 to d * 256 + 255), rows 0 and 1 name two other elements of subdomain d, row 2 names an element of subdomain d - 4 or -1, row 3 an element of subdomain d + 4 or -1. Every relation is mutual: row 0 of a names b exactly where row 1 of b names a, and row 3 of a names b exactly where row 2 of b names a. Between subdomains d and d + 4 there are 1 to 64 linked pairs, exactly 64 for some d.
All inputs are finite; a program needn't handle non-finite values. No bound on the sum of `coarse_mask` on one device may be relied on, other than what follows from the above.
Results may differ from the reference program's by a relative error of at most 0.000093.
Values sent between devices are 32-bit elements; how exact they have to be, the bound alone decides.
A program may use at most 64 MiB of HBM per device.

```python
import math
import jax
import jax.numpy as jnp
from jax import lax

NP = 512
FACE = 64
E_DEV = 256
BND = 64
CDEV = 8
GROUPS = 4
DOMAINS = 32
NE = 8192
NC = 256


def dominant_matrix(key, order, low, high, spread):
    k_diag, k_off = jax.random.split(key)
    diagonal = jnp.exp(jax.random.uniform(k_diag, (order,), jnp.float32, math.log(low), math.log(high)))
    off = jnp.clip(jax.random.normal(k_off, (order, order), jnp.float32), -4.0, 4.0)
    places = jnp.arange(order)
    on_diagonal = places[:, None] == places[None, :]
    return jnp.where(on_diagonal, diagonal[None, :], off * (spread / order ** 0.5))


def draw_stiffness(key, part):
    return dominant_matrix(jax.random.fold_in(key, 1), NP, 1.0, 3.0, 0.5)


def draw_local_inverse(key, part):
    return dominant_matrix(jax.random.fold_in(key, 2), NP, 0.4, 1.2, 0.3)


def draw_coarse_inverse(key, part):
    return dominant_matrix(jax.random.fold_in(key, 3), NC, 0.05, 0.5, 0.05)


def draw_rhs(key, part):
    k_val, k_row = jax.random.split(jax.random.fold_in(key, 4), 2)
    place = jnp.arange(NE, dtype=jnp.float32) / NE
    ramp = jnp.exp(math.log(3.0) * place)
    rows = jnp.exp(jax.random.uniform(k_row, (NE,), jnp.float32, 0.0, math.log(10.0)))
    values = jnp.clip(jax.random.normal(k_val, (NE, NP), jnp.float32), -4.0, 4.0)
    return values * (ramp * rows)[:, None]


def draw_neighbours(key, part):
    devices = NE // E_DEV
    links = devices - GROUPS
    k_cycle, k_count, k_top, k_low, k_high = jax.random.split(jax.random.fold_in(key, 5), 5)
    cycle = jax.vmap(lambda k: jax.random.permutation(k, E_DEV))(jax.random.split(k_cycle, devices)).astype(jnp.int32)
    where_in = jnp.argsort(cycle, axis=1)
    before = jnp.roll(cycle, 1, axis=1)
    after = jnp.roll(cycle, -1, axis=1)
    base = (jnp.arange(devices, dtype=jnp.int32) * E_DEV)[:, None]
    first = base + jnp.take_along_axis(before, where_in, 1)
    second = base + jnp.take_along_axis(after, where_in, 1)
    counts = jax.random.randint(k_count, (links,), 1, BND + 1)
    top = jax.random.randint(k_top, (), 0, links)
    counts = jnp.where(jnp.arange(links) == top, BND, counts)
    lower = jax.vmap(lambda k: jax.random.permutation(k, E_DEV))(jax.random.split(k_low, links)).astype(jnp.int32)
    upper = jax.vmap(lambda k: jax.random.permutation(k, E_DEV))(jax.random.split(k_high, links)).astype(jnp.int32)
    lower_rank = jnp.argsort(lower, axis=1)
    upper_rank = jnp.argsort(upper, axis=1)
    link_base = (jnp.arange(links, dtype=jnp.int32) * E_DEV)[:, None]
    partner_up = link_base + GROUPS * E_DEV + jnp.take_along_axis(upper, lower_rank, 1)
    up_side = jnp.where(lower_rank < counts[:, None], partner_up, -1)
    partner_down = link_base + jnp.take_along_axis(lower, upper_rank, 1)
    down_side = jnp.where(upper_rank < counts[:, None], partner_down, -1)
    empty = jnp.full((GROUPS, E_DEV), -1, jnp.int32)
    up_all = jnp.concatenate([up_side, empty], axis=0)
    down_all = jnp.concatenate([empty, down_side], axis=0)
    return jnp.stack([first, second, down_all, up_all]).reshape(4, NE).astype(jnp.int32)


def set_ends(result, key, low, top_value):
    spot = [jax.random.randint(jax.random.fold_in(key, axis), (), 0, length) for axis, length in enumerate(result.shape)]
    widest = result.shape.index(max(result.shape))
    next_to = spot[:widest] + [(spot[widest] + 1) % result.shape[widest]] + spot[widest + 1:]
    return result.at[tuple(spot)].set(low).at[tuple(next_to)].set(top_value)


def steps_of(rng, extent, shards, least, top_value):
    factor_of, own = 1.0, jax.random.fold_in(rng, 6)
    for dim, shards_of in shards:
        heights = jnp.exp(jax.random.uniform(jax.random.fold_in(own, dim), (shards_of,), jnp.float32, least / len(shards), top_value / len(shards)))
        factor_of = factor_of * jnp.repeat(heights, extent[dim] // shards_of).reshape([-1 if axis == dim else 1 for axis in range(len(extent))])
    return factor_of


def normal_values(key, shape, scale, reach, kind=jnp.bfloat16):
    drawn = jax.random.normal(key, shape, jnp.float32) * scale
    return jnp.minimum(jnp.maximum(drawn, -reach), reach).astype(kind)


def setup_inputs(seed: int = 0) -> dict:
    streams_of = jax.random.split(jax.random.key(seed), 10)
    rhs = draw_rhs(jax.random.fold_in(streams_of[9], 71), 0)
    kappa = jnp.clip(jnp.exp(math.log(5.0) - 2.3025851 * jax.random.uniform(streams_of[1], (NE,), jnp.float32) ** steps_of(streams_of[1], (NE,), ((0, 32),), -0.2, 0.2)), 0.5, 5.0)
    stiffness = draw_stiffness(jax.random.fold_in(streams_of[9], 71), 0)
    local_inverse = draw_local_inverse(jax.random.fold_in(streams_of[9], 71), 0)
    modes = normal_values(streams_of[4], (CDEV, NP), NP ** -0.5, 0.25, jnp.float32)
    coarse_weight = jnp.clip(0.5 + 1.0 * jax.random.uniform(streams_of[5], (CDEV, NE), jnp.float32) ** steps_of(streams_of[5], (CDEV, NE), ((1, 32),), -0.2, 0.2), 0.5, 1.5)
    coarse_mask = set_ends((jax.random.randint(streams_of[6], (CDEV, NE), 0, 2) < 1).astype(jnp.int32), jax.random.fold_in(streams_of[6], 1), 0, 1)
    coarse_inverse = draw_coarse_inverse(jax.random.fold_in(streams_of[9], 71), 0)
    neighbours = draw_neighbours(jax.random.fold_in(streams_of[9], 71), 0)
    return dict(rhs=rhs, kappa=kappa, stiffness=stiffness, local_inverse=local_inverse, modes=modes, coarse_weight=coarse_weight, coarse_mask=coarse_mask, coarse_inverse=coarse_inverse, neighbours=neighbours)


SIGMA = 1.0
HIGH = lax.Precision.HIGHEST

def operate(field, kappa, stiffness, neighbours):
    traces = jnp.concatenate([field[:, :FACE], field[:, NP - FACE:]], axis=1)
    valid = neighbours >= 0
    safe = jnp.where(valid, neighbours, 0).astype(jnp.int32)
    beside = jnp.zeros(traces.shape, jnp.float32)
    for slot in range(4):
        beside = beside + jnp.where(valid[slot][:, None], traces[safe[slot]], 0.0)
    degree = lax.optimization_barrier(jnp.sum(valid.astype(jnp.float32), axis=0))
    penalty = SIGMA * (degree[:, None] * traces - beside)
    middle = jnp.zeros((field.shape[0], NP - 2 * FACE), jnp.float32)
    lifted = jnp.concatenate([penalty[:, :FACE], middle, penalty[:, FACE:]], axis=1)
    return kappa[:, None] * jnp.dot(field, stiffness, precision=HIGH) + lifted

def precondition(residual, kappa, local_inverse, modes, weights, coarse_inverse):
    local_part = jnp.dot(residual, local_inverse, precision=HIGH) / kappa[:, None]
    projected = jnp.dot(modes, residual.T, precision=HIGH)
    restricted = lax.optimization_barrier(jnp.sum((weights * projected).reshape(CDEV, DOMAINS, E_DEV), axis=2)).T.reshape(NC)
    solved = jnp.dot(coarse_inverse, restricted, precision=HIGH)
    spread = jnp.repeat(solved.reshape(DOMAINS, CDEV).T, E_DEV, axis=1)
    coarse_part = jnp.dot((weights * spread).T, modes, precision=HIGH)
    return local_part + coarse_part

def reference(rhs, kappa, stiffness, local_inverse, modes, coarse_weight, coarse_mask, coarse_inverse, neighbours):
    weights = coarse_weight * coarse_mask.astype(jnp.float32)
    beta = jnp.sqrt(jnp.sum(rhs * rhs))
    first = rhs / beta
    z_one = precondition(first, kappa, local_inverse, modes, weights, coarse_inverse)
    w_one = operate(z_one, kappa, stiffness, neighbours)
    h11 = jnp.sum(w_one * first)
    s_one = jnp.sum(w_one * w_one)
    h21 = jnp.sqrt(s_one - h11 * h11)
    second = (w_one - h11 * first) / h21
    z_two = precondition(second, kappa, local_inverse, modes, weights, coarse_inverse)
    w_two = operate(z_two, kappa, stiffness, neighbours)
    h12 = jnp.sum(w_two * first)
    h22 = jnp.sum(w_two * second)
    s_two = jnp.sum(w_two * w_two)
    cross = h11 * h12 + h21 * h22
    det = s_one * s_two - cross * cross
    y_one = beta * (h11 * s_two - h12 * cross) / det
    y_two = beta * (h12 * s_one - h11 * cross) / det
    return y_one * z_one + y_two * z_two
```

```python
import functools

import jax
import jax.numpy as jnp
from jax import lax
from jax.experimental import pallas as pl
from jax.experimental.pallas import tpu as pltpu
from jax.sharding import PartitionSpec as P

FACE = 64
BND = 64
SIGMA = 1.0
LANES = 128
HALF = 64
MESH = pl.DeviceIdType.MESH
F32 = jnp.float32
BF16 = jnp.bfloat16


def parts(x):
    high = x.astype(BF16).astype(F32)
    return high, x - high


def dot(a, b):
    return jnp.dot(a, b, preferred_element_type=F32)


def dot_t(a, b):
    return lax.dot_general(a, b, (((1,), (1,)), ((), ())), preferred_element_type=F32)


def iota(shape, dim):
    return lax.broadcasted_iota(jnp.int32, shape, dim)


def total(x):
    return jnp.sum(jnp.sum(x, axis=0, keepdims=True), axis=1, keepdims=True)


def kernel(
    subs, groups,
    rhs_h, kappa_h, st_h, li_h, modes_h, cw_h, cm_h, ci_h, nb_h,
    out_ref,
    rhs, kappa, st, li, modes, cw, cm, nb, cx,
    msg, gbuf, hs, hbuf,
    xh, xl, lh, ll, sh, sl, p_one, p_two, acc, w_one, z_one, pen,
    lsem, gsend, grecv, hsend, hrecv, csend, crecv,
):
    n = subs * groups
    sub = lax.axis_index("sub")
    grp = lax.axis_index("grp")
    me = sub * groups + grp
    rows, width = rhs.shape
    coarse = modes.shape[0]
    nc = ci_h.shape[1]
    last = width - LANES

    loads = [
        pltpu.make_async_copy(src, dst, lsem.at[i])
        for i, (src, dst) in enumerate(
            [
                (rhs_h, rhs), (cw_h, cw), (cm_h, cm), (modes_h, modes), (li_h, li),
                (nb_h, nb), (kappa_h, kappa), (ci_h, cx.at[0, :, pl.ds(0, nc)]), (st_h, st),
            ]
        )
    ]
    for load in loads:
        load.start()

    barrier = pltpu.get_barrier_semaphore()

    def greet(i, carry):
        t = lax.rem(me + i, n)
        pl.semaphore_signal(
            barrier, inc=1, device_id=(t // groups, lax.rem(t, groups)), device_id_type=MESH
        )
        return carry

    lax.fori_loop(1, n, greet, 0)

    def share(step):
        def one(i, carry):
            t = lax.rem(me + i, n)
            pltpu.make_async_remote_copy(
                src_ref=msg.at[step],
                dst_ref=gbuf.at[step, me],
                send_sem=gsend.at[step],
                recv_sem=grecv.at[step],
                device_id=(t // groups, lax.rem(t, groups)),
                device_id_type=MESH,
            ).start()
            return carry

        lax.fori_loop(1, n, one, 0)
        gbuf[step, me] = msg[step]

    def await_all(step, sem):
        pltpu.make_async_copy(
            gbuf.at[step, pl.ds(0, n - 1)], gbuf.at[step, pl.ds(0, n - 1)], sem.at[step]
        ).wait()

    lane = iota((1, LANES), 1)
    place = lax.rem(me, 16) * coarse
    aside = HALF - HALF * lax.rem(me // 8, 2)

    def fill(step, column, scalars):
        line = jnp.zeros((1, LANES), F32)
        if column is not None:
            spot = iota((coarse, LANES), 1) == iota((coarse, LANES), 0) + place
            line = jnp.sum(jnp.where(spot, column, 0.0), axis=0, keepdims=True)
        for i, value in enumerate(scalars):
            line = line + jnp.where(lane == aside + i, value, 0.0)
        msg[step] = line

    def collect(step):
        chunks = []
        sums = jnp.zeros((1, LANES), F32)
        for c in range(n // 16):
            even = jnp.sum(gbuf[step, pl.ds(16 * c, 8)], axis=0)
            odd = jnp.sum(gbuf[step, pl.ds(16 * c + 8, 8)], axis=0)
            chunks.append(jnp.where(lane < HALF, even, odd))
            sums = sums + jnp.where(lane < HALF, odd, even)
        return chunks, sums

    def scalar(sums, i):
        return jnp.sum(
            jnp.where((lane == i) | (lane == HALF + i), sums, 0.0), axis=1, keepdims=True
        )

    for i in (0, 1, 2, 3):
        loads[i].wait()
    weights = cw[...] * cm[...].astype(F32)
    w_high, w_low = parts(weights)
    w_stack = jnp.concatenate([w_high, w_low], axis=0).astype(BF16)

    def split_to(value, high_ref, low_ref):
        high = value.astype(BF16)
        high_ref[...] = high
        low_ref[...] = (value - high.astype(F32)).astype(BF16)

    def restrict():
        both = dot(w_stack, xh[...]) + dot(w_stack, xl[...])
        return jnp.sum(
            (both[:coarse] + both[coarse:]) * modes[...], axis=1, keepdims=True
        )

    split_to(rhs[...], xh, xl)
    fill(0, restrict(), [total(rhs[...] * rhs[...])])
    pl.semaphore_wait(barrier, n - 1)
    share(0)

    up = (lax.rem(sub + 1, subs), grp)
    down = (lax.rem(sub + subs - 1, subs), grp)

    loads[5].wait()
    loads[6].wait()
    base = me * rows
    square = (rows, rows)
    across, along = iota(square, 0), iota(square, 1)
    near = jnp.where(across == nb[0:1, :] - base, 1.0, 0.0) + jnp.where(
        across == nb[1:2, :] - base, 1.0, 0.0
    )
    near = near.astype(BF16)
    below, above = nb[2:3, :].astype(F32), nb[3:4, :].astype(F32)
    degree = jnp.sum(jnp.where(nb[...] >= 0, 1.0, 0.0), axis=0, keepdims=True)
    pad = jnp.zeros((4, rows), F32)
    columns = jnp.concatenate([below, above, kappa[...], degree, pad], axis=0).T
    below_c, above_c = columns[:, 0:1], columns[:, 1:2]
    kappa_c, degree_c = columns[:, 2:3], columns[:, 3:4]
    inverse_c = 1.0 / kappa_c

    def packing(line, column):
        rank = jnp.sum(
            jnp.where((column >= 0.0) & (column < line), 1.0, 0.0), axis=0, keepdims=True
        )
        hit = (iota((BND, rows), 0).astype(F32) == rank) & (line >= 0.0)
        return jnp.where(hit, 1.0, 0.0)

    pack = jnp.concatenate([packing(above, above_c), packing(below, below_c)], axis=0).astype(BF16)
    packed = dot_t(w_stack, pack)
    cx[0, :, pl.ds(nc, LANES)] = packed[:coarse] + packed[coarse:]
    loads[7].wait()

    def coarse_copy(way, target):
        return pltpu.make_async_remote_copy(
            src_ref=cx.at[0], dst_ref=cx.at[1 + way],
            send_sem=csend.at[way], recv_sem=crecv.at[way],
            device_id=target, device_id_type=MESH,
        )

    coarse_copies = [coarse_copy(0, up), coarse_copy(1, down)]
    for copy in coarse_copies:
        copy.start()

    def rank_of(line):
        return jnp.sum(
            jnp.where((line >= 0.0) & (along < across), 1.0, 0.0), axis=1, keepdims=True
        )

    rank_below, rank_above = rank_of(below), rank_of(above)
    wide = (rows, LANES)
    lane_f = iota(wide, 1).astype(F32)
    first_half = lane_f < HALF
    put = jnp.where(
        first_half,
        jnp.where((below_c >= 0.0) & (lane_f == rank_below), 1.0, 0.0),
        jnp.where((above_c >= 0.0) & (lane_f - HALF == rank_above), 1.0, 0.0),
    ).astype(BF16)

    loads[4].wait()
    split_to(li[...], lh, ll)

    def product(high, low, m_high, m_low):
        return dot(high[...], m_high[...]) + dot(high[...], m_low[...]) + dot(low[...], m_high[...])

    def beside(matrix, value):
        high, low = parts(value)
        both = dot(matrix, jnp.concatenate([high, low], axis=1).astype(BF16))
        return both[:, :LANES] + both[:, LANES:]

    def halo_copy(step, way, target):
        block = pl.ds(BND * way, BND)
        return pltpu.make_async_remote_copy(
            src_ref=hs.at[step, block, :], dst_ref=hbuf.at[step, block, :],
            send_sem=hsend.at[step, way], recv_sem=hrecv.at[step, way],
            device_id=target, device_id_type=MESH,
        )

    def traces_of(ref):
        return jnp.where(first_half, ref[:, 0:LANES], ref[:, last:width])

    def start_local(step, ref):
        ref[...] = product(xh, xl, lh, ll) * inverse_c
        traces = traces_of(ref)
        hs[step] = beside(pack, traces)
        copies = [halo_copy(step, 0, up), halo_copy(step, 1, down)]
        for copy in copies:
            copy.start()
        return copies

    def finish_local(step, ref, copies):
        traces = traces_of(ref)
        pen[...] = degree_c * traces - beside(near, traces)
        split_to(ref[...], xh, xl)
        acc[...] = product(xh, xl, sh, sl) * kappa_c
        for copy in copies:
            copy.wait_recv()
        lifted = SIGMA * (pen[...] - beside(put, hbuf[step]))
        acc[:, 0:LANES] += jnp.where(first_half, lifted, 0.0)
        acc[:, last:width] += jnp.where(first_half, 0.0, lifted)

    halo_one = start_local(0, p_one)

    loads[8].wait()
    split_to(st[...], sh, sl)

    m_high, m_low = parts(modes[...])
    m_stack = jnp.concatenate([m_high, m_low], axis=0).astype(BF16)
    ms = dot(m_stack, sh[...]) + dot(m_stack, sl[...])
    ms = ms[:coarse] + ms[coarse:]
    column = iota((coarse, width), 1)
    faces = SIGMA * jnp.where((column < FACE) | (column >= width - FACE), modes[...], 0.0)
    linked = dot(w_stack, near)
    linked = linked[:coarse] + linked[coarse:]
    finish_local(0, p_one, halo_one)

    for copy in coarse_copies:
        copy.wait_recv()
    lane_w = iota((coarse, LANES), 1)
    from_below = jnp.where(lane_w < HALF, cx[1, :, pl.ds(nc, LANES)], 0.0)
    from_above = jnp.where(lane_w < HALF, 0.0, cx[2, :, pl.ds(nc, LANES)])
    lows, highs = parts(from_below), parts(from_above)
    outer = dot_t(
        jnp.concatenate([lows[0], highs[0], lows[1], highs[1]], axis=0).astype(BF16), put
    )
    outer = outer[: 2 * coarse] + outer[2 * coarse :]
    k_high, k_low = parts(
        jnp.concatenate([kappa[...] * weights, degree * weights - linked, -outer], axis=0)
    )
    mix = jnp.concatenate([k_high, k_low, k_high], axis=0).T.astype(BF16)
    spread = jnp.concatenate(
        [w_high, w_low, w_high, jnp.zeros_like(w_high)], axis=0
    ).T.astype(BF16)

    def stacked(value):
        high, low = parts(value)
        return [high, high, low]

    def solve(chunks):
        whole = jnp.concatenate(chunks, axis=1)
        return jnp.sum(cx[:, :, pl.ds(0, nc)] * whole[None], axis=2, keepdims=True)

    def add_to_w(y):
        own = y[0]
        values = jnp.concatenate(
            [ms * own, faces * own, faces * y[1], faces * y[2]], axis=0
        )
        return dot(mix, jnp.concatenate(stacked(values), axis=0).astype(BF16))

    def add_to_z(y):
        values = stacked(modes[...] * y[0])
        return dot(
            spread, jnp.concatenate(values + [jnp.zeros_like(values[0])], axis=0).astype(BF16)
        )

    await_all(0, grecv)
    chunks, sums = collect(0)
    beta = jnp.sqrt(scalar(sums, 0))
    scale = 1.0 / beta
    y = solve(chunks) * scale[None]
    w_one[...] = acc[...] * scale + add_to_w(y)
    split_to(w_one[...], xh, xl)
    fill(
        1,
        restrict(),
        [total(w_one[...] * rhs[...]) * scale, total(w_one[...] * w_one[...])],
    )
    share(1)

    halo_two = start_local(1, p_two)
    finish_local(1, p_two, halo_two)
    z_one[...] = p_one[...] * scale + add_to_z(y)

    await_all(1, grecv)
    chunks, sums = collect(1)
    h11 = scalar(sums, 0)
    s_one = scalar(sums, 1)
    h21 = jnp.sqrt(s_one - h11 * h11)
    over = 1.0 / h21
    y = solve(chunks)
    acc[...] = (acc[...] + add_to_w(y) - h11 * w_one[...]) * over
    first = total(acc[...] * rhs[...]) * scale
    second = total(acc[...] * (w_one[...] - (h11 * scale) * rhs[...])) * over
    third = total(acc[...] * acc[...])
    fill(2, None, [first, second, third])
    share(2)
    p_two[...] = (p_two[...] + add_to_z(y) - h11 * z_one[...]) * over

    await_all(2, grecv)
    chunks, sums = collect(2)
    h12, h22, s_two = scalar(sums, 0), scalar(sums, 1), scalar(sums, 2)
    cross = h11 * h12 + h21 * h22
    det = s_one * s_two - cross * cross
    y_one = beta * (h11 * s_two - h12 * cross) / det
    y_two = beta * (h12 * s_one - h11 * cross) / det
    out_ref[...] = y_one * z_one[...] + y_two * p_two[...]

    for step in range(3):
        await_all(step, gsend)
    for copy in coarse_copies + halo_one + halo_two:
        copy.wait_send()


def body(subs, groups, rhs, kappa, stiffness, local_inverse, modes, cw, cm, ci, nb):
    rows, width = rhs.shape
    n = subs * groups
    coarse, nc = ci.shape
    square = (width, width)
    vmem = pltpu.VMEM
    dma = pltpu.SemaphoreType.DMA
    return pl.pallas_call(
        functools.partial(kernel, subs, groups),
        out_shape=jax.ShapeDtypeStruct((rows, width), F32),
        in_specs=[pl.BlockSpec(memory_space=pl.ANY)] * 9,
        out_specs=pl.BlockSpec(memory_space=pltpu.VMEM),
        scratch_shapes=[
            vmem((rows, width), F32), vmem((1, rows), F32), vmem(square, F32), vmem(square, F32),
            vmem((coarse, width), F32), vmem((coarse, rows), F32), vmem((coarse, rows), jnp.int32),
            vmem((4, rows), jnp.int32), vmem((3, coarse, nc + LANES), F32),
            vmem((3, 1, LANES), F32), vmem((3, n, 1, LANES), F32),
            vmem((2, 2 * BND, LANES), F32), vmem((2, 2 * BND, LANES), F32),
            vmem((rows, width), BF16), vmem((rows, width), BF16),
            vmem(square, BF16), vmem(square, BF16), vmem(square, BF16), vmem(square, BF16),
            vmem((rows, width), F32), vmem((rows, width), F32), vmem((rows, width), F32),
            vmem((rows, width), F32), vmem((rows, width), F32), vmem((rows, LANES), F32),
            dma((9,)), dma((3,)), dma((3,)), dma((2, 2)), dma((2, 2)), dma((2,)), dma((2,)),
        ],
        compiler_params=pltpu.CompilerParams(
            collective_id=0, has_side_effects=True, vmem_limit_bytes=48 * 1024 * 1024
        ),
    )(rhs, kappa.reshape(1, rows), stiffness, local_inverse, modes, cw, cm, ci, nb)


def solution(mesh):
    placed = (
        P(("sub", "grp"), None),
        P(("sub", "grp")),
        P(),
        P(),
        P(),
        P(None, ("sub", "grp")),
        P(None, ("sub", "grp")),
        P(("sub", "grp"), None),
        P(None, ("sub", "grp")),
    )
    return jax.shard_map(
        functools.partial(body, mesh.shape["sub"], mesh.shape["grp"]),
        mesh=mesh, in_specs=placed, out_specs=P(("sub", "grp"), None), check_vma=False,
    )
```

```python
import functools

import jax
import jax.numpy as jnp
from jax import lax
from jax.experimental import pallas as pl
from jax.experimental.pallas import tpu as pltpu
from jax.sharding import PartitionSpec as P

FACE = 64
BND = 64
SIGMA = 1.0
LANES = 128
HALF = 64
MESH = pl.DeviceIdType.MESH
F32 = jnp.float32
BF16 = jnp.bfloat16


def parts(x):
    high = x.astype(BF16).astype(F32)
    return high, x - high


def dot(a, b):
    return jnp.dot(a, b, preferred_element_type=F32)


def dot_t(a, b):
    return lax.dot_general(a, b, (((1,), (1,)), ((), ())), preferred_element_type=F32)


def iota(shape, dim):
    return lax.broadcasted_iota(jnp.int32, shape, dim)


def total(x):
    return jnp.sum(jnp.sum(x, axis=0, keepdims=True), axis=1, keepdims=True)


def kernel(
    subs, groups,
    rhs_h, kappa_h, st_h, li_h, modes_h, cw_h, cm_h, ci_h, nb_h,
    out_ref,
    rhs, kappa, st, li, modes, cw, cm, nb, cx,
    msg, gbuf, hs, hbuf,
    xh, xl, lh, ll, sh, sl, p_one, p_two, acc, w_one, z_one, pen,
    lsem, gsend, grecv, hsend, hrecv, csend, crecv,
):
    n = subs * groups
    sub = lax.axis_index("sub")
    grp = lax.axis_index("grp")
    me = sub * groups + grp
    rows, width = rhs.shape
    coarse = modes.shape[0]
    nc = ci_h.shape[1]
    last = width - LANES

    loads = [
        pltpu.make_async_copy(src, dst, lsem.at[i])
        for i, (src, dst) in enumerate(
            [
                (rhs_h, rhs), (cw_h, cw), (cm_h, cm), (modes_h, modes), (li_h, li),
                (nb_h, nb), (kappa_h, kappa), (ci_h, cx.at[0, :, pl.ds(0, nc)]), (st_h, st),
            ]
        )
    ]
    for load in loads:
        load.start()

    barrier = pltpu.get_barrier_semaphore()

    def greet(i, carry):
        t = lax.rem(me + i, n)
        pl.semaphore_signal(
            barrier, inc=1, device_id=(t // groups, lax.rem(t, groups)), device_id_type=MESH
        )
        return carry

    lax.fori_loop(1, n, greet, 0)

    def share(step):
        def one(i, carry):
            t = lax.rem(me + i, n)
            pltpu.make_async_remote_copy(
                src_ref=msg.at[step],
                dst_ref=gbuf.at[step, me],
                send_sem=gsend.at[step],
                recv_sem=grecv.at[step],
                device_id=(t // groups, lax.rem(t, groups)),
                device_id_type=MESH,
            ).start()
            return carry

        lax.fori_loop(1, n, one, 0)
        gbuf[step, me] = msg[step]

    def await_all(step, sem):
        pltpu.make_async_copy(
            gbuf.at[step, pl.ds(0, n - 1)], gbuf.at[step, pl.ds(0, n - 1)], sem.at[step]
        ).wait()

    lane = iota((1, LANES), 1)
    place = lax.rem(me, 16) * coarse
    aside = HALF - HALF * lax.rem(me // 8, 2)

    def fill(step, column, scalars):
        line = jnp.zeros((1, LANES), F32)
        if column is not None:
            spot = iota((coarse, LANES), 1) == iota((coarse, LANES), 0) + place
            line = jnp.sum(jnp.where(spot, column, 0.0), axis=0, keepdims=True)
        for i, value in enumerate(scalars):
            line = line + jnp.where(lane == aside + i, value, 0.0)
        msg[step] = line

    def collect(step):
        chunks = []
        sums = jnp.zeros((1, LANES), F32)
        for c in range(n // 16):
            even = jnp.sum(gbuf[step, pl.ds(16 * c, 8)], axis=0)
            odd = jnp.sum(gbuf[step, pl.ds(16 * c + 8, 8)], axis=0)
            chunks.append(jnp.where(lane < HALF, even, odd))
            sums = sums + jnp.where(lane < HALF, odd, even)
        return chunks, sums

    def scalar(sums, i):
        return jnp.sum(
            jnp.where((lane == i) | (lane == HALF + i), sums, 0.0), axis=1, keepdims=True
        )

    for i in (0, 1, 2, 3):
        loads[i].wait()
    weights = cw[...] * cm[...].astype(F32)
    w_high, w_low = parts(weights)
    w_stack = jnp.concatenate([w_high, w_low], axis=0).astype(BF16)

    def split_to(value, high_ref, low_ref):
        high = value.astype(BF16)
        high_ref[...] = high
        low_ref[...] = (value - high.astype(F32)).astype(BF16)

    def restrict():
        both = dot(w_stack, xh[...]) + dot(w_stack, xl[...])
        return jnp.sum(
            (both[:coarse] + both[coarse:]) * modes[...], axis=1, keepdims=True
        )

    split_to(rhs[...], xh, xl)
    fill(0, restrict(), [total(rhs[...] * rhs[...])])
    pl.semaphore_wait(barrier, n - 1)
    share(0)

    up = (lax.rem(sub + 1, subs), grp)
    down = (lax.rem(sub + subs - 1, subs), grp)

    loads[5].wait()
    loads[6].wait()
    base = me * rows
    square = (rows, rows)
    across, along = iota(square, 0), iota(square, 1)
    near = jnp.where(across == nb[0:1, :] - base, 1.0, 0.0) + jnp.where(
        across == nb[1:2, :] - base, 1.0, 0.0
    )
    near = near.astype(BF16)
    below, above = nb[2:3, :].astype(F32), nb[3:4, :].astype(F32)
    degree = jnp.sum(jnp.where(nb[...] >= 0, 1.0, 0.0), axis=0, keepdims=True)
    pad = jnp.zeros((4, rows), F32)
    columns = jnp.concatenate([below, above, kappa[...], degree, pad], axis=0).T
    below_c, above_c = columns[:, 0:1], columns[:, 1:2]
    kappa_c, degree_c = columns[:, 2:3], columns[:, 3:4]
    inverse_c = 1.0 / kappa_c

    def packing(line, column):
        rank = jnp.sum(
            jnp.where((column >= 0.0) & (column < line), 1.0, 0.0), axis=0, keepdims=True
        )
        hit = (iota((BND, rows), 0).astype(F32) == rank) & (line >= 0.0)
        return jnp.where(hit, 1.0, 0.0)

    pack = jnp.concatenate([packing(above, above_c), packing(below, below_c)], axis=0).astype(BF16)
    packed = dot_t(w_stack, pack)
    cx[0, :, pl.ds(nc, LANES)] = packed[:coarse] + packed[coarse:]
    loads[7].wait()

    def coarse_copy(way, target):
        return pltpu.make_async_remote_copy(
            src_ref=cx.at[0], dst_ref=cx.at[1 + way],
            send_sem=csend.at[way], recv_sem=crecv.at[way],
            device_id=target, device_id_type=MESH,
        )

    coarse_copies = [coarse_copy(0, up), coarse_copy(1, down)]
    for copy in coarse_copies:
        copy.start()

    def rank_of(line):
        return jnp.sum(
            jnp.where((line >= 0.0) & (along < across), 1.0, 0.0), axis=1, keepdims=True
        )

    rank_below, rank_above = rank_of(below), rank_of(above)
    wide = (rows, LANES)
    lane_f = iota(wide, 1).astype(F32)
    first_half = lane_f < HALF
    put = jnp.where(
        first_half,
        jnp.where((below_c >= 0.0) & (lane_f == rank_below), 1.0, 0.0),
        jnp.where((above_c >= 0.0) & (lane_f - HALF == rank_above), 1.0, 0.0),
    ).astype(BF16)

    loads[4].wait()
    split_to(li[...], lh, ll)

    def product(high, low, m_high, m_low):
        return dot(high[...], m_high[...]) + dot(high[...], m_low[...]) + dot(low[...], m_high[...])

    def beside(matrix, value):
        high, low = parts(value)
        both = dot(matrix, jnp.concatenate([high, low], axis=1).astype(BF16))
        return both[:, :LANES] + both[:, LANES:]

    def halo_copy(step, way, target):
        block = pl.ds(BND * way, BND)
        return pltpu.make_async_remote_copy(
            src_ref=hs.at[step, block, :], dst_ref=hbuf.at[step, block, :],
            send_sem=hsend.at[step, way], recv_sem=hrecv.at[step, way],
            device_id=target, device_id_type=MESH,
        )

    def traces_of(ref):
        return jnp.where(first_half, ref[:, 0:LANES], ref[:, last:width])

    def start_local(step, ref):
        ref[...] = product(xh, xl, lh, ll) * inverse_c
        traces = traces_of(ref)
        hs[step] = beside(pack, traces)
        copies = [halo_copy(step, 0, up), halo_copy(step, 1, down)]
        for copy in copies:
            copy.start()
        return copies

    def finish_local(step, ref, copies):
        traces = traces_of(ref)
        pen[...] = degree_c * traces - beside(near, traces)
        split_to(ref[...], xh, xl)
        acc[...] = product(xh, xl, sh, sl) * kappa_c
        for copy in copies:
            copy.wait_recv()
        lifted = SIGMA * (pen[...] - beside(put, hbuf[step]))
        acc[:, 0:LANES] += jnp.where(first_half, lifted, 0.0)
        acc[:, last:width] += jnp.where(first_half, 0.0, lifted)

    halo_one = start_local(0, p_one)

    loads[8].wait()
    split_to(st[...], sh, sl)

    m_high, m_low = parts(modes[...])
    m_stack = jnp.concatenate([m_high, m_low], axis=0).astype(BF16)
    ms = dot(m_stack, sh[...]) + dot(m_stack, sl[...])
    ms = ms[:coarse] + ms[coarse:]
    column = iota((coarse, width), 1)
    faces = SIGMA * jnp.where((column < FACE) | (column >= width - FACE), modes[...], 0.0)
    linked = dot(w_stack, near)
    linked = linked[:coarse] + linked[coarse:]
    finish_local(0, p_one, halo_one)

    for copy in coarse_copies:
        copy.wait_recv()
    lane_w = iota((coarse, LANES), 1)
    from_below = jnp.where(lane_w < HALF, cx[1, :, pl.ds(nc, LANES)], 0.0)
    from_above = jnp.where(lane_w < HALF, 0.0, cx[2, :, pl.ds(nc, LANES)])
    lows, highs = parts(from_below), parts(from_above)
    outer = dot_t(
        jnp.concatenate([lows[0], highs[0], lows[1], highs[1]], axis=0).astype(BF16), put
    )
    outer = outer[: 2 * coarse] + outer[2 * coarse :]
    k_high, k_low = parts(
        jnp.concatenate([kappa[...] * weights, degree * weights - linked, -outer], axis=0)
    )
    mix = jnp.concatenate([k_high, k_low, k_high], axis=0).T.astype(BF16)
    spread = jnp.concatenate(
        [w_high, w_low, w_high, jnp.zeros_like(w_high)], axis=0
    ).T.astype(BF16)

    def stacked(value):
        high, low = parts(value)
        return [high, high, low]

    def solve(chunks):
        whole = jnp.concatenate(chunks, axis=1)
        return jnp.sum(cx[:, :, pl.ds(0, nc)] * whole[None], axis=2, keepdims=True)

    def add_to_w(y):
        own = y[0]
        values = jnp.concatenate(
            [ms * own, faces * own, faces * y[1], faces * y[2]], axis=0
        )
        return dot(mix, jnp.concatenate(stacked(values), axis=0).astype(BF16))

    def add_to_z(y):
        values = stacked(modes[...] * y[0])
        return dot(
            spread, jnp.concatenate(values + [jnp.zeros_like(values[0])], axis=0).astype(BF16)
        )

    await_all(0, grecv)
    chunks, sums = collect(0)
    beta = jnp.sqrt(scalar(sums, 0))
    scale = 1.0 / beta
    y = solve(chunks) * scale[None]
    w_one[...] = acc[...] * scale + add_to_w(y)
    split_to(w_one[...], xh, xl)
    fill(
        1,
        restrict(),
        [total(w_one[...] * rhs[...]) * scale, total(w_one[...] * w_one[...])],
    )
    share(1)

    halo_two = start_local(1, p_two)
    finish_local(1, p_two, halo_two)
    z_one[...] = p_one[...] * scale + add_to_z(y)

    await_all(1, grecv)
    chunks, sums = collect(1)
    h11 = scalar(sums, 0)
    s_one = scalar(sums, 1)
    h21 = jnp.sqrt(s_one - h11 * h11)
    over = 1.0 / h21
    y = solve(chunks)
    acc[...] = (acc[...] + add_to_w(y) - h11 * w_one[...]) * over
    first = total(acc[...] * rhs[...]) * scale
    second = total(acc[...] * (w_one[...] - (h11 * scale) * rhs[...])) * over
    third = total(acc[...] * acc[...])
    fill(2, None, [first, second, third])
    share(2)
    p_two[...] = (p_two[...] + add_to_z(y) - h11 * z_one[...]) * over

    await_all(2, grecv)
    chunks, sums = collect(2)
    h12, h22, s_two = scalar(sums, 0), scalar(sums, 1), scalar(sums, 2)
    cross = h11 * h12 + h21 * h22
    det = s_one * s_two - cross * cross
    y_one = beta * (h11 * s_two - h12 * cross) / det
    y_two = beta * (h12 * s_one - h11 * cross) / det
    out_ref[...] = y_one * z_one[...] + y_two * p_two[...]

    for step in range(3):
        await_all(step, gsend)
    for copy in coarse_copies + halo_one + halo_two:
        copy.wait_send()


def body(subs, groups, rhs, kappa, stiffness, local_inverse, modes, cw, cm, ci, nb):
    rows, width = rhs.shape
    n = subs * groups
    coarse, nc = ci.shape
    square = (width, width)
    vmem = pltpu.VMEM
    dma = pltpu.SemaphoreType.DMA
    return pl.pallas_call(
        functools.partial(kernel, subs, groups),
        out_shape=jax.ShapeDtypeStruct((rows, width), F32),
        in_specs=[pl.BlockSpec(memory_space=pltpu.HBM)] * 9,
        out_specs=pl.BlockSpec(memory_space=pltpu.VMEM),
        scratch_shapes=[
            vmem((rows, width), F32), vmem((1, rows), F32), vmem(square, F32), vmem(square, F32),
            vmem((coarse, width), F32), vmem((coarse, rows), F32), vmem((coarse, rows), jnp.int32),
            vmem((4, rows), jnp.int32), vmem((3, coarse, nc + LANES), F32),
            vmem((3, 1, LANES), F32), vmem((3, n, 1, LANES), F32),
            vmem((2, 2 * BND, LANES), F32), vmem((2, 2 * BND, LANES), F32),
            vmem((rows, width), BF16), vmem((rows, width), BF16),
            vmem(square, BF16), vmem(square, BF16), vmem(square, BF16), vmem(square, BF16),
            vmem((rows, width), F32), vmem((rows, width), F32), vmem((rows, width), F32),
            vmem((rows, width), F32), vmem((rows, width), F32), vmem((rows, LANES), F32),
            dma((9,)), dma((3,)), dma((3,)), dma((2, 2)), dma((2, 2)), dma((2,)), dma((2,)),
        ],
        compiler_params=pltpu.CompilerParams(
            collective_id=0, has_side_effects=True, vmem_limit_bytes=int(62 * 1024 * 1024)
        ),
    )(rhs, kappa.reshape(1, rows), stiffness, local_inverse, modes, cw, cm, ci, nb)


def solution(mesh):
    placed = (
        P(("sub", "grp"), None),
        P(("sub", "grp")),
        P(),
        P(),
        P(),
        P(None, ("sub", "grp")),
        P(None, ("sub", "grp")),
        P(("sub", "grp"), None),
        P(None, ("sub", "grp")),
    )
    return jax.shard_map(
        functools.partial(body, mesh.shape["sub"], mesh.shape["grp"]),
        mesh=mesh, in_specs=placed, out_specs=P(("sub", "grp"), None), check_vma=False,
    )
```

```python
import functools

import jax
import jax.numpy as jnp
from jax import lax
from jax.experimental import pallas as pl
from jax.experimental.pallas import tpu as pltpu
from jax.sharding import PartitionSpec as P

FACE = 64
BND = 64
SIGMA = 1.0
LANES = 128
HALF = 64
MESH = pl.DeviceIdType.MESH
F32 = jnp.float32
BF16 = jnp.bfloat16


def parts(x):
    high = x.astype(BF16).astype(F32)
    return high, x - high


def dot(a, b):
    return jnp.dot(a, b, preferred_element_type=F32)


def dot_t(a, b):
    return lax.dot_general(a, b, (((1,), (1,)), ((), ())), preferred_element_type=F32)


def iota(shape, dim):
    return lax.broadcasted_iota(jnp.int32, shape, dim)


def total(x):
    return jnp.sum(jnp.sum(x, axis=0, keepdims=True), axis=1, keepdims=True)


def kernel(
    subs, groups,
    rhs_h, kappa_h, st_h, li_h, modes_h, cw_h, cm_h, ci_h, nb_h,
    out_ref,
    rhs, kappa, st, li, modes, cw, cm, nb, cx,
    msg, gbuf, hs, hbuf,
    xh, xl, lh, ll, sh, sl, p_one, p_two, acc, w_one, z_one, pen,
    lsem, gsend, grecv, hsend, hrecv, csend, crecv,
):
    n = subs * groups
    sub = lax.axis_index("sub")
    grp = lax.axis_index("grp")
    me = sub * groups + grp
    rows, width = rhs.shape
    coarse = modes.shape[0]
    nc = ci_h.shape[1]
    last = width - LANES

    loads = [
        pltpu.make_async_copy(src, dst, lsem.at[i])
        for i, (src, dst) in enumerate(
            [
                (rhs_h, rhs), (cw_h, cw), (cm_h, cm), (modes_h, modes), (li_h, li),
                (nb_h, nb), (kappa_h, kappa), (ci_h, cx.at[0, :, pl.ds(0, nc)]), (st_h, st),
            ]
        )
    ]
    for load in loads:
        load.start()

    barrier = pltpu.get_barrier_semaphore()

    peers = [lax.rem(grp + j, groups) for j in range(groups)]

    def each_other(act):
        def plane(i, carry):
            other = lax.rem(sub + i, subs)
            for peer in peers:
                act((other, peer))
            return carry

        if subs <= 8:
            for i in sorted(range(1, subs), key=lambda i: abs(i - subs // 2)):
                plane(i, 0)
        else:
            lax.fori_loop(1, subs, plane, 0)
        for peer in peers[1:]:
            act((sub, peer))

    each_other(
        lambda target: pl.semaphore_signal(
            barrier, inc=1, device_id=target, device_id_type=MESH
        )
    )
    has_up, has_down = sub < subs - 1, sub > 0

    @pl.when(sub == 0)
    def _():
        hbuf[:, 0:BND, :] = jnp.zeros((2, BND, LANES), F32)
        cx[1] = jnp.zeros(cx.shape[1:], F32)

    @pl.when(sub == subs - 1)
    def _():
        hbuf[:, BND:, :] = jnp.zeros((2, BND, LANES), F32)
        cx[2] = jnp.zeros(cx.shape[1:], F32)

    def share(step):
        each_other(
            lambda target: pltpu.make_async_remote_copy(
                src_ref=msg.at[step],
                dst_ref=gbuf.at[step, me],
                send_sem=gsend.at[step],
                recv_sem=grecv.at[step],
                device_id=target,
                device_id_type=MESH,
            ).start()
        )
        gbuf[step, me] = msg[step]

    def await_all(step, sem):
        pltpu.make_async_copy(
            gbuf.at[step, pl.ds(0, n - 1)], gbuf.at[step, pl.ds(0, n - 1)], sem.at[step]
        ).wait()

    lane = iota((1, LANES), 1)
    place = lax.rem(me, 16) * coarse
    aside = HALF - HALF * lax.rem(me // 8, 2)

    def fill(step, column, scalars):
        line = jnp.zeros((1, LANES), F32)
        if column is not None:
            spot = iota((coarse, LANES), 1) == iota((coarse, LANES), 0) + place
            line = jnp.sum(jnp.where(spot, column, 0.0), axis=0, keepdims=True)
        for i, value in enumerate(scalars):
            line = line + jnp.where(lane == aside + i, value, 0.0)
        msg[step] = line

    def collect(step):
        chunks = []
        sums = jnp.zeros((1, LANES), F32)
        for c in range(n // 16):
            even = jnp.sum(gbuf[step, pl.ds(16 * c, 8)], axis=0)
            odd = jnp.sum(gbuf[step, pl.ds(16 * c + 8, 8)], axis=0)
            chunks.append(jnp.where(lane < HALF, even, odd))
            sums = sums + jnp.where(lane < HALF, odd, even)
        return chunks, sums

    def scalar(sums, i):
        return jnp.sum(
            jnp.where((lane == i) | (lane == HALF + i), sums, 0.0), axis=1, keepdims=True
        )

    for i in (0, 1, 2, 3):
        loads[i].wait()
    weights = cw[...] * cm[...].astype(F32)
    w_high, w_low = parts(weights)
    w_stack = jnp.concatenate([w_high, w_low], axis=0).astype(BF16)

    def split_to(value, high_ref, low_ref):
        high = value.astype(BF16)
        high_ref[...] = high
        low_ref[...] = (value - high.astype(F32)).astype(BF16)

    def restrict():
        both = dot(w_stack, xh[...]) + dot(w_stack, xl[...])
        return jnp.sum(
            (both[:coarse] + both[coarse:]) * modes[...], axis=1, keepdims=True
        )

    split_to(rhs[...], xh, xl)
    fill(0, restrict(), [total(rhs[...] * rhs[...])])
    pl.semaphore_wait(barrier, n - 1)
    share(0)

    up = (lax.rem(sub + 1, subs), grp)
    down = (lax.rem(sub + subs - 1, subs), grp)

    loads[5].wait()
    loads[6].wait()
    base = me * rows
    square = (rows, rows)
    across, along = iota(square, 0), iota(square, 1)
    near = jnp.where(across == nb[0:1, :] - base, 1.0, 0.0) + jnp.where(
        across == nb[1:2, :] - base, 1.0, 0.0
    )
    near = near.astype(BF16)
    below, above = nb[2:3, :].astype(F32), nb[3:4, :].astype(F32)
    degree = jnp.sum(jnp.where(nb[...] >= 0, 1.0, 0.0), axis=0, keepdims=True)
    pad = jnp.zeros((4, rows), F32)
    columns = jnp.concatenate([below, above, kappa[...], degree, pad], axis=0).T
    below_c, above_c = columns[:, 0:1], columns[:, 1:2]
    kappa_c, degree_c = columns[:, 2:3], columns[:, 3:4]
    inverse_c = 1.0 / kappa_c

    def packing(line, column):
        rank = jnp.sum(
            jnp.where((column >= 0.0) & (column < line), 1.0, 0.0), axis=0, keepdims=True
        )
        hit = (iota((BND, rows), 0).astype(F32) == rank) & (line >= 0.0)
        return jnp.where(hit, 1.0, 0.0)

    pack = jnp.concatenate([packing(above, above_c), packing(below, below_c)], axis=0).astype(BF16)
    packed = dot_t(w_stack, pack)
    cx[0, :, pl.ds(nc, LANES)] = packed[:coarse] + packed[coarse:]
    loads[7].wait()

    def coarse_copy(way, target):
        return pltpu.make_async_remote_copy(
            src_ref=cx.at[0], dst_ref=cx.at[1 + way],
            send_sem=csend.at[way], recv_sem=crecv.at[way],
            device_id=target, device_id_type=MESH,
        )

    def start(copies):
        pl.when(has_up)(copies[0].start)
        pl.when(has_down)(copies[1].start)

    def arrive(copies):
        pl.when(has_down)(copies[0].wait_recv)
        pl.when(has_up)(copies[1].wait_recv)

    def leave(copies):
        pl.when(has_up)(copies[0].wait_send)
        pl.when(has_down)(copies[1].wait_send)

    coarse_copies = [coarse_copy(0, up), coarse_copy(1, down)]
    start(coarse_copies)

    def rank_of(line):
        return jnp.sum(
            jnp.where((line >= 0.0) & (along < across), 1.0, 0.0), axis=1, keepdims=True
        )

    rank_below, rank_above = rank_of(below), rank_of(above)
    wide = (rows, LANES)
    lane_f = iota(wide, 1).astype(F32)
    first_half = lane_f < HALF
    put = jnp.where(
        first_half,
        jnp.where((below_c >= 0.0) & (lane_f == rank_below), 1.0, 0.0),
        jnp.where((above_c >= 0.0) & (lane_f - HALF == rank_above), 1.0, 0.0),
    ).astype(BF16)

    loads[4].wait()
    split_to(li[...], lh, ll)

    def product(high, low, m_high, m_low):
        return dot(high[...], m_high[...]) + dot(high[...], m_low[...]) + dot(low[...], m_high[...])

    def beside(matrix, value):
        high, low = parts(value)
        both = dot(matrix, jnp.concatenate([high, low], axis=1).astype(BF16))
        return both[:, :LANES] + both[:, LANES:]

    def halo_copy(step, way, target):
        block = pl.ds(BND * way, BND)
        return pltpu.make_async_remote_copy(
            src_ref=hs.at[step, block, :], dst_ref=hbuf.at[step, block, :],
            send_sem=hsend.at[step, way], recv_sem=hrecv.at[step, way],
            device_id=target, device_id_type=MESH,
        )

    def traces_of(ref):
        return jnp.where(first_half, ref[:, 0:LANES], ref[:, last:width])

    def start_local(step, ref):
        ref[...] = product(xh, xl, lh, ll) * inverse_c
        traces = traces_of(ref)
        hs[step] = beside(pack, traces)
        copies = [halo_copy(step, 0, up), halo_copy(step, 1, down)]
        start(copies)
        return copies

    def finish_local(step, ref, copies):
        traces = traces_of(ref)
        pen[...] = degree_c * traces - beside(near, traces)
        split_to(ref[...], xh, xl)
        acc[...] = product(xh, xl, sh, sl) * kappa_c
        arrive(copies)
        lifted = SIGMA * (pen[...] - beside(put, hbuf[step]))
        acc[:, 0:LANES] += jnp.where(first_half, lifted, 0.0)
        acc[:, last:width] += jnp.where(first_half, 0.0, lifted)

    halo_one = start_local(0, p_one)

    loads[8].wait()
    split_to(st[...], sh, sl)

    m_high, m_low = parts(modes[...])
    m_stack = jnp.concatenate([m_high, m_low], axis=0).astype(BF16)
    ms = dot(m_stack, sh[...]) + dot(m_stack, sl[...])
    ms = ms[:coarse] + ms[coarse:]
    column = iota((coarse, width), 1)
    faces = SIGMA * jnp.where((column < FACE) | (column >= width - FACE), modes[...], 0.0)
    linked = dot(w_stack, near)
    linked = linked[:coarse] + linked[coarse:]
    finish_local(0, p_one, halo_one)

    arrive(coarse_copies)
    lane_w = iota((coarse, LANES), 1)
    from_below = jnp.where(lane_w < HALF, cx[1, :, pl.ds(nc, LANES)], 0.0)
    from_above = jnp.where(lane_w < HALF, 0.0, cx[2, :, pl.ds(nc, LANES)])
    lows, highs = parts(from_below), parts(from_above)
    outer = dot_t(
        jnp.concatenate([lows[0], highs[0], lows[1], highs[1]], axis=0).astype(BF16), put
    )
    outer = outer[: 2 * coarse] + outer[2 * coarse :]
    k_high, k_low = parts(
        jnp.concatenate([kappa[...] * weights, degree * weights - linked, -outer], axis=0)
    )
    mix = jnp.concatenate([k_high, k_low, k_high], axis=0).T.astype(BF16)
    spread = jnp.concatenate(
        [w_high, w_low, w_high, jnp.zeros_like(w_high)], axis=0
    ).T.astype(BF16)

    def stacked(value):
        high, low = parts(value)
        return [high, high, low]

    def solve(chunks):
        whole = jnp.concatenate(chunks, axis=1)
        return jnp.sum(cx[:, :, pl.ds(0, nc)] * whole[None], axis=2, keepdims=True)

    def add_to_w(y):
        own = y[0]
        values = jnp.concatenate(
            [ms * own, faces * own, faces * y[1], faces * y[2]], axis=0
        )
        return dot(mix, jnp.concatenate(stacked(values), axis=0).astype(BF16))

    def add_to_z(y):
        values = stacked(modes[...] * y[0])
        return dot(
            spread, jnp.concatenate(values + [jnp.zeros_like(values[0])], axis=0).astype(BF16)
        )

    await_all(0, grecv)
    chunks, sums = collect(0)
    beta = jnp.sqrt(scalar(sums, 0))
    scale = 1.0 / beta
    y = solve(chunks) * scale[None]
    w_one[...] = acc[...] * scale + add_to_w(y)
    split_to(w_one[...], xh, xl)
    fill(
        1,
        restrict(),
        [total(w_one[...] * rhs[...]) * scale, total(w_one[...] * w_one[...])],
    )
    share(1)

    halo_two = start_local(1, p_two)
    finish_local(1, p_two, halo_two)
    z_one[...] = p_one[...] * scale + add_to_z(y)

    await_all(1, grecv)
    chunks, sums = collect(1)
    h11 = scalar(sums, 0)
    s_one = scalar(sums, 1)
    h21 = jnp.sqrt(s_one - h11 * h11)
    over = 1.0 / h21
    y = solve(chunks)
    acc[...] = (acc[...] + add_to_w(y) - h11 * w_one[...]) * over
    first = total(acc[...] * rhs[...]) * scale
    second = total(acc[...] * (w_one[...] - (h11 * scale) * rhs[...])) * over
    third = total(acc[...] * acc[...])
    fill(2, None, [first, second, third])
    share(2)
    p_two[...] = (p_two[...] + add_to_z(y) - h11 * z_one[...]) * over

    await_all(2, grecv)
    chunks, sums = collect(2)
    h12, h22, s_two = scalar(sums, 0), scalar(sums, 1), scalar(sums, 2)
    cross = h11 * h12 + h21 * h22
    det = s_one * s_two - cross * cross
    y_one = beta * (h11 * s_two - h12 * cross) / det
    y_two = beta * (h12 * s_one - h11 * cross) / det
    out_ref[...] = y_one * z_one[...] + y_two * p_two[...]

    for step in range(3):
        await_all(step, gsend)
    for copies in (coarse_copies, halo_one, halo_two):
        leave(copies)


def body(subs, groups, rhs, kappa, stiffness, local_inverse, modes, cw, cm, ci, nb):
    rows, width = rhs.shape
    n = subs * groups
    coarse, nc = ci.shape
    square = (width, width)
    vmem = pltpu.VMEM
    dma = pltpu.SemaphoreType.DMA
    return pl.pallas_call(
        functools.partial(kernel, subs, groups),
        out_shape=jax.ShapeDtypeStruct((rows, width), F32),
        in_specs=[pl.BlockSpec(memory_space=pltpu.HBM)] * 9,
        out_specs=pl.BlockSpec(memory_space=pltpu.VMEM),
        scratch_shapes=[
            vmem((rows, width), F32), vmem((1, rows), F32), vmem(square, F32), vmem(square, F32),
            vmem((coarse, width), F32), vmem((coarse, rows), F32), vmem((coarse, rows), jnp.int32),
            vmem((4, rows), jnp.int32), vmem((3, coarse, nc + LANES), F32),
            vmem((3, 1, LANES), F32), vmem((3, n, 1, LANES), F32),
            vmem((2, 2 * BND, LANES), F32), vmem((2, 2 * BND, LANES), F32),
            vmem((rows, width), BF16), vmem((rows, width), BF16),
            vmem(square, BF16), vmem(square, BF16), vmem(square, BF16), vmem(square, BF16),
            vmem((rows, width), F32), vmem((rows, width), F32), vmem((rows, width), F32),
            vmem((rows, width), F32), vmem((rows, width), F32), vmem((rows, LANES), F32),
            dma((9,)), dma((3,)), dma((3,)), dma((2, 2)), dma((2, 2)), dma((2,)), dma((2,)),
        ],
        compiler_params=pltpu.CompilerParams(
            collective_id=0, has_side_effects=True, vmem_limit_bytes=int(62 * 1024 * 1024)
        ),
    )(rhs, kappa.reshape(1, rows), stiffness, local_inverse, modes, cw, cm, ci, nb)


def solution(mesh):
    placed = (
        P(("sub", "grp"), None),
        P(("sub", "grp")),
        P(),
        P(),
        P(),
        P(None, ("sub", "grp")),
        P(None, ("sub", "grp")),
        P(("sub", "grp"), None),
        P(None, ("sub", "grp")),
    )
    return jax.shard_map(
        functools.partial(body, mesh.shape["sub"], mesh.shape["grp"]),
        mesh=mesh, in_specs=placed, out_specs=P(("sub", "grp"), None), check_vma=False,
    )
```

```python
import functools

import jax
import jax.numpy as jnp
from jax import lax
from jax.experimental import pallas as pl
from jax.experimental.pallas import tpu as pltpu
from jax.sharding import PartitionSpec as P

FACE = 64
BND = 64
SIGMA = 1.0
LANES = 128
HALF = 64
MESH = pl.DeviceIdType.MESH
F32 = jnp.float32
BF16 = jnp.bfloat16


def parts(x):
    high = x.astype(BF16).astype(F32)
    return high, x - high


def dot(a, b):
    return jnp.dot(a, b, preferred_element_type=F32)


def dot_t(a, b):
    return lax.dot_general(a, b, (((1,), (1,)), ((), ())), preferred_element_type=F32)


def iota(shape, dim):
    return lax.broadcasted_iota(jnp.int32, shape, dim)


def total(x):
    return jnp.sum(jnp.sum(x, axis=0, keepdims=True), axis=1, keepdims=True)


def kernel(
    subs, groups,
    rhs_h, kappa_h, st_h, li_h, modes_h, cw_h, cm_h, ci_h, nb_h,
    out_ref,
    rhs, kappa, st, li, modes, cw, cm, nb, cx,
    msg, merged, gbuf, sbuf, hs, hbuf,
    xh, xl, lh, ll, sh, sl, p_one, p_two, acc, w_one, z_one, pen,
    lsem, gsend, grecv, hsend, hrecv, csend, crecv,
):
    n = subs * groups
    sub = lax.axis_index("sub")
    grp = lax.axis_index("grp")
    me = sub * groups + grp
    rows, width = rhs.shape
    coarse = modes.shape[0]
    nc = ci_h.shape[1]
    last = width - LANES

    loads = [
        pltpu.make_async_copy(src, dst, lsem.at[i])
        for i, (src, dst) in enumerate(
            [
                (rhs_h, rhs), (cw_h, cw), (cm_h, cm), (modes_h, modes), (li_h, li),
                (nb_h, nb), (kappa_h, kappa), (ci_h, cx.at[0, :, pl.ds(0, nc)]), (st_h, st),
            ]
        )
    ]
    for load in loads:
        load.start()

    barrier = pltpu.get_barrier_semaphore()

    def each_in_group(act):
        for i in range(1, groups):
            act((sub, lax.rem(grp + i, groups)))

    def each_in_stack(act):
        def one(i, carry):
            act((lax.rem(sub + i, subs), grp))
            return carry

        if subs <= 8:
            for i in sorted(range(1, subs), key=lambda i: abs(i - subs // 2)):
                one(i, 0)
        else:
            lax.fori_loop(1, subs, one, 0)

    for each in (each_in_stack, each_in_group):
        each(
            lambda target: pl.semaphore_signal(
                barrier, inc=1, device_id=target, device_id_type=MESH
            )
        )
    has_up, has_down = sub < subs - 1, sub > 0

    @pl.when(sub == 0)
    def _():
        hbuf[:, 0:BND, :] = jnp.zeros((2, BND, LANES), F32)
        cx[1] = jnp.zeros(cx.shape[1:], F32)

    @pl.when(sub == subs - 1)
    def _():
        hbuf[:, BND:, :] = jnp.zeros((2, BND, LANES), F32)
        cx[2] = jnp.zeros(cx.shape[1:], F32)

    def send(step, stage, each, lines, place_of, slot):
        each(
            lambda target: pltpu.make_async_remote_copy(
                src_ref=lines.at[step],
                dst_ref=place_of.at[step, slot],
                send_sem=gsend.at[step, stage],
                recv_sem=grecv.at[step, stage],
                device_id=target,
                device_id_type=MESH,
            ).start()
        )
        place_of[step, slot] = lines[step]

    def await_all(step, stage, sem):
        place_of, count = (gbuf, groups) if stage == 0 else (sbuf, subs)
        block = place_of.at[step, pl.ds(0, count - 1)]
        pltpu.make_async_copy(block, block, sem.at[step, stage]).wait()

    def share(step):
        send(step, 0, each_in_group, msg, gbuf, grp)

    def pass_on(step):
        await_all(step, 0, grecv)
        merged[step] = jnp.sum(gbuf[step], axis=0)
        send(step, 1, each_in_stack, merged, sbuf, sub)

    lane = iota((1, LANES), 1)
    place = lax.rem(me, 16) * coarse
    aside = HALF - HALF * lax.rem(me // 8, 2)

    def fill(step, column, scalars):
        line = jnp.zeros((1, LANES), F32)
        if column is not None:
            spot = iota((coarse, LANES), 1) == iota((coarse, LANES), 0) + place
            line = jnp.sum(jnp.where(spot, column, 0.0), axis=0, keepdims=True)
        for i, value in enumerate(scalars):
            line = line + jnp.where(lane == aside + i, value, 0.0)
        msg[step] = line

    def collect(step):
        chunks = []
        sums = jnp.zeros((1, LANES), F32)
        per = 8 // groups
        for c in range(n // 16):
            even = jnp.sum(sbuf[step, pl.ds(2 * per * c, per)], axis=0)
            odd = jnp.sum(sbuf[step, pl.ds(2 * per * c + per, per)], axis=0)
            chunks.append(jnp.where(lane < HALF, even, odd))
            sums = sums + jnp.where(lane < HALF, odd, even)
        return chunks, sums

    def scalar(sums, i):
        return jnp.sum(
            jnp.where((lane == i) | (lane == HALF + i), sums, 0.0), axis=1, keepdims=True
        )

    for i in (0, 1, 2, 3):
        loads[i].wait()
    weights = cw[...] * cm[...].astype(F32)
    w_high, w_low = parts(weights)
    w_stack = jnp.concatenate([w_high, w_low], axis=0).astype(BF16)

    def split_to(value, high_ref, low_ref):
        high = value.astype(BF16)
        high_ref[...] = high
        low_ref[...] = (value - high.astype(F32)).astype(BF16)

    def restrict():
        both = dot(w_stack, xh[...]) + dot(w_stack, xl[...])
        return jnp.sum(
            (both[:coarse] + both[coarse:]) * modes[...], axis=1, keepdims=True
        )

    split_to(rhs[...], xh, xl)
    fill(0, restrict(), [total(rhs[...] * rhs[...])])
    pl.semaphore_wait(barrier, groups + subs - 2)
    share(0)

    up = (lax.rem(sub + 1, subs), grp)
    down = (lax.rem(sub + subs - 1, subs), grp)

    loads[5].wait()
    loads[6].wait()
    base = me * rows
    square = (rows, rows)
    across, along = iota(square, 0), iota(square, 1)
    near = jnp.where(across == nb[0:1, :] - base, 1.0, 0.0) + jnp.where(
        across == nb[1:2, :] - base, 1.0, 0.0
    )
    near = near.astype(BF16)
    below, above = nb[2:3, :].astype(F32), nb[3:4, :].astype(F32)
    degree = jnp.sum(jnp.where(nb[...] >= 0, 1.0, 0.0), axis=0, keepdims=True)
    pad = jnp.zeros((4, rows), F32)
    columns = jnp.concatenate([below, above, kappa[...], degree, pad], axis=0).T
    below_c, above_c = columns[:, 0:1], columns[:, 1:2]
    kappa_c, degree_c = columns[:, 2:3], columns[:, 3:4]
    inverse_c = 1.0 / kappa_c

    def packing(line, column):
        rank = jnp.sum(
            jnp.where((column >= 0.0) & (column < line), 1.0, 0.0), axis=0, keepdims=True
        )
        hit = (iota((BND, rows), 0).astype(F32) == rank) & (line >= 0.0)
        return jnp.where(hit, 1.0, 0.0)

    pack = jnp.concatenate([packing(above, above_c), packing(below, below_c)], axis=0).astype(BF16)
    packed = dot_t(w_stack, pack)
    cx[0, :, pl.ds(nc, LANES)] = packed[:coarse] + packed[coarse:]
    loads[7].wait()

    def coarse_copy(way, target):
        return pltpu.make_async_remote_copy(
            src_ref=cx.at[0], dst_ref=cx.at[1 + way],
            send_sem=csend.at[way], recv_sem=crecv.at[way],
            device_id=target, device_id_type=MESH,
        )

    def start(copies):
        pl.when(has_up)(copies[0].start)
        pl.when(has_down)(copies[1].start)

    def arrive(copies):
        pl.when(has_down)(copies[0].wait_recv)
        pl.when(has_up)(copies[1].wait_recv)

    def leave(copies):
        pl.when(has_up)(copies[0].wait_send)
        pl.when(has_down)(copies[1].wait_send)

    coarse_copies = [coarse_copy(0, up), coarse_copy(1, down)]
    start(coarse_copies)

    def rank_of(line):
        return jnp.sum(
            jnp.where((line >= 0.0) & (along < across), 1.0, 0.0), axis=1, keepdims=True
        )

    rank_below, rank_above = rank_of(below), rank_of(above)
    wide = (rows, LANES)
    lane_f = iota(wide, 1).astype(F32)
    first_half = lane_f < HALF
    put = jnp.where(
        first_half,
        jnp.where((below_c >= 0.0) & (lane_f == rank_below), 1.0, 0.0),
        jnp.where((above_c >= 0.0) & (lane_f - HALF == rank_above), 1.0, 0.0),
    ).astype(BF16)

    loads[4].wait()
    split_to(li[...], lh, ll)

    def product(high, low, m_high, m_low):
        return dot(high[...], m_high[...]) + dot(high[...], m_low[...]) + dot(low[...], m_high[...])

    def beside(matrix, value):
        high, low = parts(value)
        both = dot(matrix, jnp.concatenate([high, low], axis=1).astype(BF16))
        return both[:, :LANES] + both[:, LANES:]

    def halo_copy(step, way, target):
        block = pl.ds(BND * way, BND)
        return pltpu.make_async_remote_copy(
            src_ref=hs.at[step, block, :], dst_ref=hbuf.at[step, block, :],
            send_sem=hsend.at[step, way], recv_sem=hrecv.at[step, way],
            device_id=target, device_id_type=MESH,
        )

    def traces_of(ref):
        return jnp.where(first_half, ref[:, 0:LANES], ref[:, last:width])

    def start_local(step, ref):
        ref[...] = product(xh, xl, lh, ll) * inverse_c
        traces = traces_of(ref)
        hs[step] = beside(pack, traces)
        copies = [halo_copy(step, 0, up), halo_copy(step, 1, down)]
        start(copies)
        return copies

    def finish_local(step, ref, copies):
        traces = traces_of(ref)
        pen[...] = degree_c * traces - beside(near, traces)
        split_to(ref[...], xh, xl)
        acc[...] = product(xh, xl, sh, sl) * kappa_c
        arrive(copies)
        lifted = SIGMA * (pen[...] - beside(put, hbuf[step]))
        acc[:, 0:LANES] += jnp.where(first_half, lifted, 0.0)
        acc[:, last:width] += jnp.where(first_half, 0.0, lifted)

    halo_one = start_local(0, p_one)
    pass_on(0)

    loads[8].wait()
    split_to(st[...], sh, sl)

    m_high, m_low = parts(modes[...])
    m_stack = jnp.concatenate([m_high, m_low], axis=0).astype(BF16)
    ms = dot(m_stack, sh[...]) + dot(m_stack, sl[...])
    ms = ms[:coarse] + ms[coarse:]
    column = iota((coarse, width), 1)
    faces = SIGMA * jnp.where((column < FACE) | (column >= width - FACE), modes[...], 0.0)
    linked = dot(w_stack, near)
    linked = linked[:coarse] + linked[coarse:]
    finish_local(0, p_one, halo_one)

    arrive(coarse_copies)
    lane_w = iota((coarse, LANES), 1)
    from_below = jnp.where(lane_w < HALF, cx[1, :, pl.ds(nc, LANES)], 0.0)
    from_above = jnp.where(lane_w < HALF, 0.0, cx[2, :, pl.ds(nc, LANES)])
    lows, highs = parts(from_below), parts(from_above)
    outer = dot_t(
        jnp.concatenate([lows[0], highs[0], lows[1], highs[1]], axis=0).astype(BF16), put
    )
    outer = outer[: 2 * coarse] + outer[2 * coarse :]
    k_high, k_low = parts(
        jnp.concatenate([kappa[...] * weights, degree * weights - linked, -outer], axis=0)
    )
    mix = jnp.concatenate([k_high, k_low, k_high], axis=0).T.astype(BF16)
    spread = jnp.concatenate(
        [w_high, w_low, w_high, jnp.zeros_like(w_high)], axis=0
    ).T.astype(BF16)

    def stacked(value):
        high, low = parts(value)
        return [high, high, low]

    def solve(chunks):
        whole = jnp.concatenate(chunks, axis=1)
        return jnp.sum(cx[:, :, pl.ds(0, nc)] * whole[None], axis=2, keepdims=True)

    def add_to_w(y):
        own = y[0]
        values = jnp.concatenate(
            [ms * own, faces * own, faces * y[1], faces * y[2]], axis=0
        )
        return dot(mix, jnp.concatenate(stacked(values), axis=0).astype(BF16))

    def add_to_z(y):
        values = stacked(modes[...] * y[0])
        return dot(
            spread, jnp.concatenate(values + [jnp.zeros_like(values[0])], axis=0).astype(BF16)
        )

    await_all(0, 1, grecv)
    chunks, sums = collect(0)
    beta = jnp.sqrt(scalar(sums, 0))
    scale = 1.0 / beta
    y = solve(chunks) * scale[None]
    w_one[...] = acc[...] * scale + add_to_w(y)
    split_to(w_one[...], xh, xl)
    fill(
        1,
        restrict(),
        [total(w_one[...] * rhs[...]) * scale, total(w_one[...] * w_one[...])],
    )
    share(1)

    halo_two = start_local(1, p_two)
    pass_on(1)
    finish_local(1, p_two, halo_two)
    z_one[...] = p_one[...] * scale + add_to_z(y)

    await_all(1, 1, grecv)
    chunks, sums = collect(1)
    h11 = scalar(sums, 0)
    s_one = scalar(sums, 1)
    h21 = jnp.sqrt(s_one - h11 * h11)
    over = 1.0 / h21
    y = solve(chunks)
    acc[...] = (acc[...] + add_to_w(y) - h11 * w_one[...]) * over
    first = total(acc[...] * rhs[...]) * scale
    second = total(acc[...] * (w_one[...] - (h11 * scale) * rhs[...])) * over
    third = total(acc[...] * acc[...])
    fill(2, None, [first, second, third])
    share(2)
    p_two[...] = (p_two[...] + add_to_z(y) - h11 * z_one[...]) * over
    pass_on(2)

    await_all(2, 1, grecv)
    chunks, sums = collect(2)
    h12, h22, s_two = scalar(sums, 0), scalar(sums, 1), scalar(sums, 2)
    cross = h11 * h12 + h21 * h22
    det = s_one * s_two - cross * cross
    y_one = beta * (h11 * s_two - h12 * cross) / det
    y_two = beta * (h12 * s_one - h11 * cross) / det
    out_ref[...] = y_one * z_one[...] + y_two * p_two[...]

    for step in range(3):
        for stage in range(2):
            await_all(step, stage, gsend)
    for copies in (coarse_copies, halo_one, halo_two):
        leave(copies)


def body(subs, groups, rhs, kappa, stiffness, local_inverse, modes, cw, cm, ci, nb):
    rows, width = rhs.shape
    coarse, nc = ci.shape
    square = (width, width)
    vmem = pltpu.VMEM
    dma = pltpu.SemaphoreType.DMA
    return pl.pallas_call(
        functools.partial(kernel, subs, groups),
        out_shape=jax.ShapeDtypeStruct((rows, width), F32),
        in_specs=[pl.BlockSpec(memory_space=pltpu.HBM)] * 9,
        out_specs=pl.BlockSpec(memory_space=pltpu.VMEM),
        scratch_shapes=[
            vmem((rows, width), F32), vmem((1, rows), F32), vmem(square, F32), vmem(square, F32),
            vmem((coarse, width), F32), vmem((coarse, rows), F32), vmem((coarse, rows), jnp.int32),
            vmem((4, rows), jnp.int32), vmem((3, coarse, nc + LANES), F32),
            vmem((3, 1, LANES), F32), vmem((3, 1, LANES), F32),
            vmem((3, groups, 1, LANES), F32), vmem((3, subs, 1, LANES), F32),
            vmem((2, 2 * BND, LANES), F32), vmem((2, 2 * BND, LANES), F32),
            vmem((rows, width), BF16), vmem((rows, width), BF16),
            vmem(square, BF16), vmem(square, BF16), vmem(square, BF16), vmem(square, BF16),
            vmem((rows, width), F32), vmem((rows, width), F32), vmem((rows, width), F32),
            vmem((rows, width), F32), vmem((rows, width), F32), vmem((rows, LANES), F32),
            dma((9,)), dma((3, 2)), dma((3, 2)), dma((2, 2)), dma((2, 2)), dma((2,)), dma((2,)),
        ],
        compiler_params=pltpu.CompilerParams(
            collective_id=0, has_side_effects=True, vmem_limit_bytes=int(62 * 1024 * 1024)
        ),
    )(rhs, kappa.reshape(1, rows), stiffness, local_inverse, modes, cw, cm, ci, nb)


def solution(mesh):
    placed = (
        P(("sub", "grp"), None),
        P(("sub", "grp")),
        P(),
        P(),
        P(),
        P(None, ("sub", "grp")),
        P(None, ("sub", "grp")),
        P(("sub", "grp"), None),
        P(None, ("sub", "grp")),
    )
    return jax.shard_map(
        functools.partial(body, mesh.shape["sub"], mesh.shape["grp"]),
        mesh=mesh, in_specs=placed, out_specs=P(("sub", "grp"), None), check_vma=False,
    )
```
